32 devices in a mesh: groups: 2 (over y), pool: 4 (over z), ffn: 2 (over x), sub: 2 (over core).
Axes of the slice: x: 2, y: 2, z: 4, core: 2. Of those that a mesh axis runs over, the one named last changes fastest.
Arguments:
- queries: bfloat16 [256, 8192], P(('groups', 'pool'), ('ffn', 'sub')), parts along dimension 0, may hold values from -200 to 200
- cache_keys: bfloat16 [256, 128, 1024], P(('groups', 'pool'), None, ('ffn', 'sub')), parts along dimension 0, may hold values from -6 to 6
- cache_values: bfloat16 [256, 128, 1024], P(('groups', 'pool'), None, ('ffn', 'sub')), parts along dimension 0, may hold values from -6 to 6
- new_keys: bfloat16 [256, 1024], P(('groups', 'pool'), ('ffn', 'sub')), parts along dimension 0, may hold values from -6 to 6
- new_values: bfloat16 [256, 1024], P(('groups', 'pool'), ('ffn', 'sub')), parts along dimension 0, may hold values from -6 to 6
- kv_lengths: int32 [256], P(('groups', 'pool')), parts along dimension 0, may hold values from 1 to 128, 8192 in all
- residual: float32 [256, 8192], P(('groups', 'pool'), ('ffn', 'sub')), parts along dimension 0, may hold values from -200 to 200
- norm_gain: float32 [8192], P(('ffn', 'sub')), may hold values from 0.1 to 1.9
- gate_weight: bfloat16 [8192, 14336], P(('ffn', 'sub'), 'pool'), may hold values from -0.0625 to 0.0625
- up_weight: bfloat16 [8192, 14336], P(('ffn', 'sub'), 'pool'), may hold values from -0.0625 to 0.0625
- down_weight: bfloat16 [14336, 8192], P('pool', ('ffn', 'sub')), may hold values from -0.046875 to 0.046875
Outputs:
- layer_out: float32 [256, 8192], P(('groups', 'pool'), ('ffn', 'sub')), parts along dimension 0
The draws below stay inside these ranges and needn't reach their ends.
There are 2 independent parts, one for each index of `groups`. The reference program is written for one: setup_inputs(seed, part) draws one part's arguments, and reference() takes and returns one part's arrays. A program takes and returns all parts, laid end to end along the dimension named above; an argument that names none is the same for every part. Nothing has to cross between parts.
Inputs may be any that keep to these rules, and one draw needn't show every extreme that they name: `kv_lengths`: the lengths of one part sum to 128 * 128 // 2 (the total is per part, not over all parts).
All inputs are finite; a program needn't handle non-finite values. No bound on the sum of `kv_lengths` on one device may be relied on, other than what follows from the above.
Results may differ from the reference program's by a relative error of at most 0.0035.
Values may be sent and summed in bfloat16 or wider, within the bound.
A program may use at most 128 MiB of HBM per device.

```python
import math
import jax
import jax.numpy as jnp
import numpy as np
from jax import lax

QHEADS = 64
KVHEADS = 8
HEAD_DIM = 128
D = 8192
FF = 14336
CAP = 128
ROWS = 128
N_POOL = 4
N_FFN = 2
N_SUB = 2


def shared_keys(key):
    return jax.random.truncated_normal(key, -6.0, 6.0, (ROWS, CAP, KVHEADS * HEAD_DIM), jnp.float32)


def draw_cache_keys(key, part):
    key_draw = shared_keys(key)
    return key_draw.astype(jnp.bfloat16)


def draw_queries(key, part):
    key = jax.random.fold_in(key, 5)
    return jax.random.truncated_normal(key, -6.0, 6.0, (ROWS, QHEADS * HEAD_DIM), jnp.float32).astype(jnp.bfloat16)


def draw_residual(key, part):
    key = jax.random.fold_in(key, 7)
    key_list = jax.random.split(key, 3)
    basis = jax.random.truncated_normal(key_list[0], -6.0, 6.0, (ROWS, D), jnp.float32)
    row_scale = jnp.exp(jax.random.uniform(key_list[1], (ROWS, 1), jnp.float32, 0.0, math.log(10.0)))
    ramp = 1.0 + 2.0 * jnp.arange(D, dtype=jnp.float32)[None, :] / (D - 1)
    column_scale = jnp.exp(jax.random.uniform(key_list[2], (1, D), jnp.float32, 0.0, math.log(10.0))) * ramp
    return 0.1 * basis * row_scale * column_scale


def level_of(rng, dims, shards, least, high):
    gain = 1.0
    for position, parts in shards:
        heights = jax.random.uniform(jax.random.fold_in(jax.random.fold_in(rng, 6), position), (parts,), jnp.float32, least / len(shards), high / len(shards))
        gain = gain * jnp.repeat(jnp.exp(heights), dims[position] // parts).reshape((-1,) + (1,) * (len(dims) - 1 - position))
    return gain


def length_profile(number_of, total, most, lean):
    weights = [(1 << 20) // math.isqrt(rank ** lean) + 1 for rank in range(2, number_of + 1)]
    rest, holding = total - most - (number_of - 1), [1] * (number_of - 1)
    while rest > 0:
        movable = [i for i in range(number_of - 1) if holding[i] < most]
        pool, left = sum([weights[i] for i in movable]), rest
        for i in movable:
            extra = min(most - holding[i], max(1, left * weights[i] // pool), rest)
            holding[i] = holding[i] + extra
            rest = rest - extra
    return np.array([most] + holding)


def ragged(stream_key, number_of, total, limit, skew):
    if number_of == 2:
        one = jax.random.randint(stream_key, (), max(1, total - limit), min(limit, total - 1) + 1)
        return jnp.stack([one, total - one])
    lengths = jnp.asarray(length_profile(number_of, total, limit, skew), jnp.int32)
    twos = (number_of - 1) // 2
    source_of, taker = lengths[1:1 + 2 * twos:2], lengths[2:2 + 2 * twos:2]
    slack = jnp.minimum(source_of - 1, limit - taker)
    shifted = jax.random.randint(jax.random.fold_in(stream_key, 1), (twos,), 0, 1 << 20) % (slack + 1)
    lengths = lengths.at[1:1 + 2 * twos:2].set(source_of - shifted).at[2:2 + 2 * twos:2].set(taker + shifted)
    return lengths[jax.random.permutation(jax.random.fold_in(stream_key, 2), number_of)]


def noise(own_key, shape, width, bound, pieces=(), kind=jnp.bfloat16):
    array = width * jax.random.normal(own_key, shape, jnp.float32)
    if pieces:
        array = array * level_of(own_key, shape, pieces, -0.22, 0.18)
    return jnp.clip(array, -bound, bound).astype(kind)


def setup_inputs(seed: int = 0, part: int = 0) -> dict:
    arg_keys = jax.random.split(jax.random.key(seed), 12)
    own_keys = jax.random.split(jax.random.fold_in(arg_keys[11], part), 12)
    return {
        "queries": draw_queries(jax.random.fold_in(jax.random.fold_in(arg_keys[11], part), 71), part),
        "cache_keys": draw_cache_keys(jax.random.fold_in(jax.random.fold_in(arg_keys[11], part), 71), part),
        "cache_values": noise(own_keys[2], (ROWS, CAP, KVHEADS * HEAD_DIM), 1.0, 6.0, ((0, 4), (2, 4))),
        "new_keys": noise(own_keys[3], (ROWS, KVHEADS * HEAD_DIM), 1.0, 6.0, ((0, 4), (1, 4))),
        "new_values": noise(own_keys[4], (ROWS, KVHEADS * HEAD_DIM), 1.0, 6.0, ((0, 4), (1, 4))),
        "kv_lengths": ragged(own_keys[5], ROWS, ROWS * CAP // 2, CAP, 2).astype(jnp.int32),
        "residual": draw_residual(jax.random.fold_in(jax.random.fold_in(arg_keys[11], part), 71), part),
        "norm_gain": jnp.clip(1.0 + 0.18 * jax.random.normal(arg_keys[7], (D,), jnp.float32), 0.1, 1.9),
        "gate_weight": noise(arg_keys[8], (D, FF), D ** -0.5, 0.0625, ((0, 4), (1, 4))),
        "up_weight": noise(arg_keys[9], (D, FF), D ** -0.5, 0.0625, ((0, 4), (1, 4))),
        "down_weight": noise(arg_keys[10], (FF, D), FF ** -0.5, 0.046875, ((0, 4), (1, 4))),
    }


def rounded(values):
    return lax.optimization_barrier(values.astype(jnp.bfloat16)).astype(jnp.float32)

def reference(queries, cache_keys, cache_values, new_keys, new_values, kv_lengths, residual, norm_gain, gate_weight, up_weight, down_weight):
    group_size = QHEADS // KVHEADS
    scaling = 1.0 / math.sqrt(HEAD_DIM)
    positions = jnp.arange(CAP, dtype=jnp.int32)
    live_mask = positions[None, :] < kv_lengths.astype(jnp.int32)[:, None]
    outputs = []
    for head_index in range(KVHEADS):
        q_lo = head_index * group_size * HEAD_DIM
        q_hi = q_lo + group_size * HEAD_DIM
        k_lo = head_index * HEAD_DIM
        k_hi = k_lo + HEAD_DIM
        query_block = queries[:, q_lo:q_hi].astype(jnp.float32).reshape(ROWS, group_size, HEAD_DIM)
        key_block = cache_keys[:, :, k_lo:k_hi].astype(jnp.float32)
        value_block = cache_values[:, :, k_lo:k_hi].astype(jnp.float32)
        scores = jnp.einsum('rgd,rcd->rgc', query_block, key_block) * scaling
        self_score = jnp.einsum('rgd,rd->rg', query_block, new_keys[:, k_lo:k_hi].astype(jnp.float32)) * scaling
        scores = jnp.where(live_mask[:, None, :], scores, -jnp.inf)
        largest = jnp.maximum(lax.optimization_barrier(jnp.max(scores, axis=2)), self_score)
        expo = jnp.exp(scores - largest[:, :, None])
        self_expo = jnp.exp(self_score - largest)
        totals = lax.optimization_barrier(jnp.sum(expo, axis=2)) + self_expo
        weights = rounded(expo)
        self_weight = rounded(self_expo)
        mixed = jnp.einsum('rgc,rcd->rgd', weights, value_block)
        mixed = mixed + self_weight[:, :, None] * new_values[:, k_lo:k_hi].astype(jnp.float32)[:, None, :]
        outputs.append((mixed / totals[:, :, None]).reshape(ROWS, group_size * HEAD_DIM))
    attended = jnp.concatenate(outputs, axis=1)
    hidden_state = residual + attended
    mean_square = lax.optimization_barrier(jnp.sum(hidden_state * hidden_state, axis=1)) / D
    normed = (hidden_state * lax.rsqrt(mean_square + 1e-05)[:, None] * norm_gain[None, :]).astype(jnp.bfloat16)
    feature_split = N_FFN * N_SUB
    feature_width = D // feature_split
    gate_total = jnp.zeros((ROWS, FF), jnp.float32)
    up_total = jnp.zeros((ROWS, FF), jnp.float32)
    for slice_index in range(feature_split):
        low = slice_index * feature_width
        high = low + feature_width
        gate_total = gate_total + rounded(jnp.dot(normed[:, low:high], gate_weight[low:high], preferred_element_type=jnp.float32))
        up_total = up_total + rounded(jnp.dot(normed[:, low:high], up_weight[low:high], preferred_element_type=jnp.float32))
    hidden_units = (jax.nn.silu(gate_total) * up_total).astype(jnp.bfloat16)
    unit_width = FF // N_POOL
    ffn_total = jnp.zeros((ROWS, D), jnp.float32)
    for pool_index in range(N_POOL):
        low = pool_index * unit_width
        high = low + unit_width
        ffn_total = ffn_total + rounded(jnp.dot(hidden_units[:, low:high], down_weight[low:high], preferred_element_type=jnp.float32))
    return hidden_state + ffn_total
```

```python
import functools
import math

import jax
import jax.numpy as jnp
from jax import lax
from jax.experimental import pallas as pl
from jax.experimental.pallas import tpu as pltpu
from jax.sharding import PartitionSpec as P

HEAD_DIM = 128
D = 8192
MESH = pl.DeviceIdType.MESH
VMEM_BYTES = 60 * 1024 * 1024


def rounded(values):
    return lax.optimization_barrier(values.astype(jnp.bfloat16)).astype(jnp.float32)


def attend(queries, cache_keys, cache_values, new_keys, new_values, kv_lengths):
    row_count, cap_len, kv_width = cache_keys.shape
    kv_local = kv_width // HEAD_DIM
    group_size = queries.shape[1] // kv_width
    scaling = 1.0 / math.sqrt(HEAD_DIM)
    query_heads = queries.reshape(row_count, kv_local, group_size, HEAD_DIM)
    key_heads = cache_keys.reshape(row_count, cap_len, kv_local, HEAD_DIM)
    value_heads = cache_values.reshape(row_count, cap_len, kv_local, HEAD_DIM)
    scores = (
        jnp.einsum("rhgd,rchd->rhgc", query_heads, key_heads, preferred_element_type=jnp.float32)
        * scaling
    )
    self_score = (
        jnp.einsum(
            "rhgd,rhd->rhg",
            query_heads,
            new_keys.reshape(row_count, kv_local, HEAD_DIM),
            preferred_element_type=jnp.float32,
        )
        * scaling
    )
    live_mask = lax.broadcasted_iota(jnp.int32, (row_count, cap_len), 1) < kv_lengths[:, None]
    scores = jnp.where(live_mask[:, None, None, :], scores, -jnp.inf)
    largest = jnp.maximum(jnp.max(scores, axis=3), self_score)
    expo = jnp.exp(scores - largest[..., None])
    self_expo = jnp.exp(self_score - largest)
    totals = jnp.sum(expo, axis=3) + self_expo
    mixed = jnp.einsum(
        "rhgc,rchd->rhgd",
        expo.astype(jnp.bfloat16),
        value_heads,
        preferred_element_type=jnp.float32,
    )
    mixed = mixed + rounded(self_expo)[..., None] * new_values.reshape(
        row_count, kv_local, 1, HEAD_DIM
    ).astype(jnp.float32)
    return (mixed / totals[..., None]).reshape(row_count, kv_local * group_size * HEAD_DIM)


def layer_rows(
    queries,
    cache_keys,
    cache_values,
    new_keys,
    new_values,
    kv_lengths,
    residual,
    norm_gain,
    gate_weight,
    up_weight,
    down_weight,
):
    hidden_state = residual + attend(
        queries, cache_keys, cache_values, new_keys, new_values, kv_lengths
    )
    squares = lax.psum(jnp.sum(hidden_state * hidden_state, axis=1), ("ffn", "sub"))
    normed = (hidden_state * lax.rsqrt(squares / D + 1e-05)[:, None] * norm_gain[None, :]).astype(
        jnp.bfloat16
    )
    unit_width = gate_weight.shape[1]
    block_rows = lax.all_gather(normed, "pool", axis=0, tiled=True)
    gate_part = jnp.dot(block_rows, gate_weight, preferred_element_type=jnp.float32)
    up_part = jnp.dot(block_rows, up_weight, preferred_element_type=jnp.float32)
    partial_value = jnp.concatenate([gate_part, up_part], axis=1)
    summed = lax.psum(partial_value.astype(jnp.bfloat16), ("ffn", "sub")).astype(jnp.float32)
    hidden_units = (jax.nn.silu(summed[:, :unit_width]) * summed[:, unit_width:]).astype(
        jnp.bfloat16
    )
    ffn_total = lax.psum_scatter(
        jnp.dot(hidden_units, down_weight, preferred_element_type=jnp.float32).astype(jnp.bfloat16),
        "pool",
        scatter_dimension=0,
        tiled=True,
    ).astype(jnp.float32)
    return hidden_state + ffn_total


def fused_kernel(
    n_pool,
    q_hbm, k_hbm, v_hbm, nk_ref, nv_ref, len_ref, res_hbm, gain_ref, g_hbm, u_hbm, d_hbm,
    out_ref,
    qbuf, kbuf, vbuf, res, gw, uw, dw,
    qs, nkx, nvx, att, hid, xall, sqp, sqall,
    s1, r1, s2, r2, s3, r3, hall, acc, dsend, drecv,
    in_sem, w_sem, xs_sem, xr_sem, qs_sem, qr_sem, ts_sem, tr_sem,
    ps_sem, pr_sem, hs_sem, hr_sem, ds_sem, dr_sem,
):
    rows, width = qbuf.shape
    cap_len = kbuf.shape[1]
    kv_local = kbuf.shape[2] // HEAD_DIM
    heads = width // HEAD_DIM
    group_size = heads // kv_local
    units = hall.shape[2]
    half = rows // 2
    scaling = 1.0 / math.sqrt(HEAD_DIM)
    f32, bf16 = jnp.float32, jnp.bfloat16

    p = lax.axis_index("pool")
    f = lax.axis_index("ffn")
    s = lax.axis_index("sub")
    me = f * 2 + s
    pool_at = [lax.rem(p + d, n_pool) for d in range(1, n_pool)]
    sibling = {"sub": 1 - s}
    across = {"ffn": 1 - f}
    diagonal = {"ffn": 1 - f, "sub": 1 - s}
    near = [sibling, across, diagonal]

    def remote(src, dst, send, recv, to):
        return pltpu.make_async_remote_copy(
            src_ref=src, dst_ref=dst, send_sem=send, recv_sem=recv,
            device_id=to, device_id_type=MESH,
        )

    early = [
        pltpu.make_async_copy(q_hbm, qbuf, in_sem.at[0]),
        pltpu.make_async_copy(res_hbm, res, in_sem.at[1]),
    ]
    caches = []
    for c in range(2):
        at = pl.ds(c * half, half)
        caches.append(
            [
                pltpu.make_async_copy(k_hbm.at[at], kbuf.at[at], in_sem.at[2 + 2 * c]),
                pltpu.make_async_copy(v_hbm.at[at], vbuf.at[at], in_sem.at[3 + 2 * c]),
            ]
        )
    for copy in early + caches[0] + caches[1]:
        copy.start()
    weights = []
    for i, (src, dst) in enumerate(((g_hbm, gw), (u_hbm, uw), (d_hbm, dw))):
        step = src.shape[0] // 4
        weights.append(
            [
                pltpu.make_async_copy(
                    src.at[pl.ds(t * step, step)], dst.at[pl.ds(t * step, step)], w_sem.at[i, t]
                )
                for t in range(4)
            ]
        )

    barrier = pltpu.get_barrier_semaphore()
    for to in near + [{"pool": t} for t in pool_at]:
        pl.semaphore_signal(barrier, inc=1, device_id=to, device_id_type=MESH)

    for copy in early:
        copy.wait()
    for h in range(heads):
        kv = h // group_size
        qs[:, h, :] = qbuf[:, h * HEAD_DIM : (h + 1) * HEAD_DIM].astype(f32)
        nkx[:, h, :] = nk_ref[:, kv * HEAD_DIM : (kv + 1) * HEAD_DIM].astype(f32)
        nvx[:, h, :] = nv_ref[:, kv * HEAD_DIM : (kv + 1) * HEAD_DIM].astype(f32)

    batch = 8
    head_row = lax.broadcasted_iota(jnp.int32, (heads, HEAD_DIM), 0) // group_size
    lane = lax.broadcasted_iota(jnp.int32, (heads, cap_len), 1)

    def attend_batch(first):
        q3 = qs[pl.ds(first, batch)]
        self_score = jnp.sum(q3 * nkx[pl.ds(first, batch)], axis=2, keepdims=True) * scaling
        scores = []
        for b in range(batch):
            q = q3[b].astype(bf16)
            zero = jnp.zeros_like(q)
            wide = jnp.concatenate(
                [jnp.where(head_row == kv, q, zero) for kv in range(kv_local)], axis=1
            )
            raw = lax.dot_general(
                wide, kbuf[first + b], (((1,), (1,)), ((), ())), preferred_element_type=f32
            )
            scores.append(jnp.where(lane < len_ref[first + b], raw * scaling, -jnp.inf))
        scores = jnp.stack(scores)
        largest = jnp.maximum(jnp.max(scores, axis=2, keepdims=True), self_score)
        expo = jnp.exp(scores - largest)
        self_expo = jnp.exp(self_score - largest)
        totals = jnp.sum(expo, axis=2, keepdims=True) + self_expo
        weight = expo.astype(bf16)
        self_weight = self_expo.astype(bf16).astype(f32)
        mixed = []
        for b in range(batch):
            wide = jnp.dot(weight[b], vbuf[first + b], preferred_element_type=f32)
            one = wide[:, :HEAD_DIM]
            for kv in range(1, kv_local):
                one = jnp.where(
                    head_row == kv, wide[:, kv * HEAD_DIM : (kv + 1) * HEAD_DIM], one
                )
            mixed.append(one)
        mixed = jnp.stack(mixed) + self_weight * nvx[pl.ds(first, batch)]
        att[pl.ds(first, batch)] = mixed / totals

    gathers = []
    for c in range(2):
        for copy in caches[c]:
            copy.wait()
        for copy in weights[c]:
            copy.start()

        @pl.loop(0, half // batch)
        def _(i):
            attend_batch(c * half + i * batch)

        at = pl.ds(c * half, half)
        mine = pl.ds(pl.multiple_of(p * rows + c * half, half), half)
        squares = jnp.zeros((half, HEAD_DIM), f32)
        for h in range(heads):
            cols = pl.ds(h * HEAD_DIM, HEAD_DIM)
            state = res[at, cols] + att[at, h, :]
            hid[at, cols] = state
            squares = squares + state * state
            xall[mine, cols] = (state * gain_ref[:, cols]).astype(bf16)
        sqp[me, at] = jnp.broadcast_to(
            jnp.sum(squares, axis=1, keepdims=True), (half, HEAD_DIM)
        )
        if c == 0:
            pl.semaphore_wait(barrier, 3 + n_pool - 1)
        for d, to in enumerate(pool_at):
            copy = remote(
                xall.at[mine], xall.at[mine], xs_sem.at[c, d], xr_sem.at[c, d], {"pool": to}
            )
            copy.start()
            gathers.append(copy)
    for copy in weights[2]:
        copy.start()

    parts_sent = [
        remote(sqp.at[me], sqp.at[me], qs_sem.at[i], qr_sem.at[i], to)
        for i, to in enumerate(near)
    ]
    for copy in parts_sent:
        copy.start()
    for copy in parts_sent:
        copy.wait()
    sqall[p] = sqp[0] + sqp[1] + sqp[2] + sqp[3]
    sums_sent = [
        remote(sqall.at[p], sqall.at[p], ts_sem.at[d], tr_sem.at[d], {"pool": to})
        for d, to in enumerate(pool_at)
    ]
    for copy in sums_sent:
        copy.start()

    for w in weights[:2]:
        for copy in w:
            copy.wait()
    for copy in gathers:
        copy.wait()

    def part(w, j):
        return jnp.dot(
            xall[...],
            w[:, pl.ds(pl.multiple_of(j * units, HEAD_DIM), units)],
            preferred_element_type=f32,
        )

    held = []
    pair = (gw, uw)
    for c in range(2):
        s1[c] = part(pair[c], 3 - me).astype(bf16)
        first = remote(s1.at[c], r1.at[c], ps_sem.at[0, c], pr_sem.at[0, c], sibling)
        first.start()
        value = part(pair[c], (1 - f) * 2 + s)
        first.wait()
        s2[c] = (value.astype(bf16).astype(f32) + r1[c].astype(f32)).astype(bf16)
        second = remote(s2.at[c], r2.at[c], ps_sem.at[1, c], pr_sem.at[1, c], across)
        second.start()
        held.append(second)
    for c in range(2):
        s3[c] = part(pair[c], f * 2 + 1 - s).astype(bf16)
        third = remote(s3.at[c], r3.at[c], ps_sem.at[2, c], pr_sem.at[2, c], sibling)
        third.start()
        held.append(third)
    own = [part(pair[c], me) for c in range(2)]
    for copy in sums_sent:
        copy.wait()
    scale = lax.rsqrt(sqall[...].reshape(n_pool * rows, HEAD_DIM)[:, :1] / D + 1e-05)
    for copy in held:
        copy.wait()
    gate, up = [
        (own[c].astype(bf16).astype(f32) + r3[c].astype(f32) + r2[c].astype(f32)) * scale
        for c in range(2)
    ]
    hall[me] = (gate / (1.0 + jnp.exp(-gate)) * up).astype(bf16)

    to_across = remote(hall.at[me], hall.at[me], hs_sem.at[0], hr_sem.at[0], across)
    to_sibling = remote(hall.at[me], hall.at[me], hs_sem.at[1], hr_sem.at[1], sibling)
    to_across.start()
    to_sibling.start()
    for copy in weights[2]:
        copy.wait()
    tile = 512

    def down(j, cols):
        return jnp.dot(
            hall[j],
            dw[pl.ds(pl.multiple_of(j * units, HEAD_DIM), units), cols],
            preferred_element_type=f32,
        )

    def column(i):
        return pl.ds(pl.multiple_of(i * tile, tile), tile)

    @pl.loop(0, width // tile)
    def _(i):
        acc[:, column(i)] = down(me, column(i))

    to_sibling.wait()

    @pl.loop(0, width // tile)
    def _(i):
        acc[:, column(i)] += down(f * 2 + 1 - s, column(i))

    to_across.wait()
    other = (1 - f) * 2 + s
    passed = remote(hall.at[other], hall.at[other], hs_sem.at[2], hr_sem.at[2], sibling)
    passed.start()

    @pl.loop(0, width // tile)
    def _(i):
        acc[:, column(i)] += down(other, column(i))

    passed.wait()
    scattered = []
    pieces = width // tile
    for i in range(pieces):
        cols = pl.ds(i * tile, tile)
        dsend[:, cols] = (acc[:, cols] + down(3 - me, cols)).astype(bf16)
        for d, to in enumerate(pool_at):
            copy = remote(
                dsend.at[pl.ds(pl.multiple_of(to * rows, rows), rows), cols],
                drecv.at[p, :, cols],
                ds_sem.at[i, d], dr_sem.at[i, d], {"pool": to},
            )
            copy.start()
            scattered.append(copy)
    drecv[p] = dsend[pl.ds(pl.multiple_of(p * rows, rows), rows), :]
    for i in range(pieces):
        cols = pl.ds(i * tile, tile)
        for copy in scattered[i * (n_pool - 1) : (i + 1) * (n_pool - 1)]:
            copy.wait()
        total = drecv[0, :, cols].astype(f32)
        for k in range(1, n_pool):
            total = total + drecv[k, :, cols].astype(f32)
        out_ref[:, cols] = hid[:, cols] + total


def fused_rows(
    n_pool, queries, cache_keys, cache_values, new_keys, new_values, kv_lengths,
    residual, norm_gain, gate_weight, up_weight, down_weight,
):
    rows, width = queries.shape
    every = n_pool * rows
    unit_width = gate_weight.shape[1]
    units = unit_width // 4
    heads = width // HEAD_DIM
    f32, bf16 = jnp.float32, jnp.bfloat16
    anywhere = pl.BlockSpec(memory_space=pl.ANY)
    vmem = pl.BlockSpec(memory_space=pltpu.VMEM)
    smem = pl.BlockSpec(memory_space=pltpu.SMEM)
    per_head = pltpu.VMEM((rows, heads, HEAD_DIM), f32)
    pair = pltpu.VMEM((2, every, units), bf16)
    dma = pltpu.SemaphoreType.DMA
    far = n_pool - 1
    return pl.pallas_call(
        functools.partial(fused_kernel, n_pool),
        out_shape=jax.ShapeDtypeStruct((rows, width), f32),
        in_specs=[anywhere] * 3 + [vmem] * 2 + [smem, anywhere, vmem] + [anywhere] * 3,
        out_specs=vmem,
        scratch_shapes=[
            pltpu.VMEM(queries.shape, bf16),
            pltpu.VMEM(cache_keys.shape, bf16),
            pltpu.VMEM(cache_values.shape, bf16),
            pltpu.VMEM(residual.shape, f32),
            pltpu.VMEM(gate_weight.shape, bf16),
            pltpu.VMEM(up_weight.shape, bf16),
            pltpu.VMEM(down_weight.shape, bf16),
            per_head, per_head, per_head, per_head,
            pltpu.VMEM((rows, width), f32),
            pltpu.VMEM((every, width), bf16),
            pltpu.VMEM((4, rows, HEAD_DIM), f32),
            pltpu.VMEM((n_pool, rows, HEAD_DIM), f32),
            pair, pair, pair, pair, pair, pair,
            pltpu.VMEM((4, every, units), bf16),
            pltpu.VMEM((every, width), f32),
            pltpu.VMEM((every, width), bf16),
            pltpu.VMEM((n_pool, rows, width), bf16),
            dma((6,)), dma((3, 4)),
            dma((2, far)), dma((2, far)), dma((3,)), dma((3,)), dma((far,)), dma((far,)),
            dma((3, 2)), dma((3, 2)), dma((3,)), dma((3,)),
            dma((width // 512, far)), dma((width // 512, far)),
        ],
        compiler_params=pltpu.CompilerParams(
            collective_id=0, has_side_effects=True, vmem_limit_bytes=VMEM_BYTES
        ),
    )(
        queries, cache_keys, cache_values, new_keys, new_values, kv_lengths, residual,
        norm_gain.reshape(1, width), gate_weight, up_weight, down_weight,
    )


def fits(n_pool, n_ffn, n_sub, queries, cache_keys, gate_weight, down_weight):
    rows, width = queries.shape
    unit_width = gate_weight.shape[1]
    weight_bytes = 2 * (2 * gate_weight.size + down_weight.size)
    return (
        n_ffn == 2
        and n_sub == 2
        and n_pool > 1
        and rows % 32 == 0
        and width % 512 == 0
        and unit_width % (4 * HEAD_DIM) == 0
        and weight_bytes + 4 * cache_keys.size + 24 * n_pool * rows * unit_width
        <= VMEM_BYTES
    )


def on_device(mesh_shape, *operands):
    n_pool, n_ffn, n_sub = mesh_shape["pool"], mesh_shape["ffn"], mesh_shape["sub"]
    queries, cache_keys = operands[0], operands[1]
    if fits(n_pool, n_ffn, n_sub, queries, cache_keys, operands[8], operands[10]):
        return fused_rows(n_pool, *operands)
    return layer_rows(*operands)


def solution(mesh):
    placed = (
        P(("groups", "pool"), ("ffn", "sub")),
        P(("groups", "pool"), None, ("ffn", "sub")),
        P(("groups", "pool"), None, ("ffn", "sub")),
        P(("groups", "pool"), ("ffn", "sub")),
        P(("groups", "pool"), ("ffn", "sub")),
        P(("groups", "pool")),
        P(("groups", "pool"), ("ffn", "sub")),
        P(("ffn", "sub")),
        P(("ffn", "sub"), "pool"),
        P(("ffn", "sub"), "pool"),
        P("pool", ("ffn", "sub")),
    )
    return jax.shard_map(
        functools.partial(on_device, dict(mesh.shape)),
        mesh=mesh,
        in_specs=placed,
        out_specs=P(("groups", "pool"), ("ffn", "sub")),
        check_vma=False,
    )
```

```python
import functools
import math

import jax
import jax.numpy as jnp
from jax import lax
from jax.experimental import pallas as pl
from jax.experimental.pallas import tpu as pltpu
from jax.sharding import PartitionSpec as P

HEAD_DIM = 128
D = 8192
MESH = pl.DeviceIdType.MESH
VMEM_BYTES = 60 * 1024 * 1024


def rounded(values):
    return lax.optimization_barrier(values.astype(jnp.bfloat16)).astype(jnp.float32)


def attend(queries, cache_keys, cache_values, new_keys, new_values, kv_lengths):
    row_count, cap_len, kv_width = cache_keys.shape
    kv_local = kv_width // HEAD_DIM
    group_size = queries.shape[1] // kv_width
    scaling = 1.0 / math.sqrt(HEAD_DIM)
    query_heads = queries.reshape(row_count, kv_local, group_size, HEAD_DIM)
    key_heads = cache_keys.reshape(row_count, cap_len, kv_local, HEAD_DIM)
    value_heads = cache_values.reshape(row_count, cap_len, kv_local, HEAD_DIM)
    scores = (
        jnp.einsum("rhgd,rchd->rhgc", query_heads, key_heads, preferred_element_type=jnp.float32)
        * scaling
    )
    self_score = (
        jnp.einsum(
            "rhgd,rhd->rhg",
            query_heads,
            new_keys.reshape(row_count, kv_local, HEAD_DIM),
            preferred_element_type=jnp.float32,
        )
        * scaling
    )
    live_mask = lax.broadcasted_iota(jnp.int32, (row_count, cap_len), 1) < kv_lengths[:, None]
    scores = jnp.where(live_mask[:, None, None, :], scores, -jnp.inf)
    largest = jnp.maximum(jnp.max(scores, axis=3), self_score)
    expo = jnp.exp(scores - largest[..., None])
    self_expo = jnp.exp(self_score - largest)
    totals = jnp.sum(expo, axis=3) + self_expo
    mixed = jnp.einsum(
        "rhgc,rchd->rhgd",
        expo.astype(jnp.bfloat16),
        value_heads,
        preferred_element_type=jnp.float32,
    )
    mixed = mixed + rounded(self_expo)[..., None] * new_values.reshape(
        row_count, kv_local, 1, HEAD_DIM
    ).astype(jnp.float32)
    return (mixed / totals[..., None]).reshape(row_count, kv_local * group_size * HEAD_DIM)


def layer_rows(
    queries,
    cache_keys,
    cache_values,
    new_keys,
    new_values,
    kv_lengths,
    residual,
    norm_gain,
    gate_weight,
    up_weight,
    down_weight,
):
    hidden_state = residual + attend(
        queries, cache_keys, cache_values, new_keys, new_values, kv_lengths
    )
    squares = lax.psum(jnp.sum(hidden_state * hidden_state, axis=1), ("ffn", "sub"))
    normed = (hidden_state * lax.rsqrt(squares / D + 1e-05)[:, None] * norm_gain[None, :]).astype(
        jnp.bfloat16
    )
    unit_width = gate_weight.shape[1]
    block_rows = lax.all_gather(normed, "pool", axis=0, tiled=True)
    gate_part = jnp.dot(block_rows, gate_weight, preferred_element_type=jnp.float32)
    up_part = jnp.dot(block_rows, up_weight, preferred_element_type=jnp.float32)
    partial_value = jnp.concatenate([gate_part, up_part], axis=1)
    summed = lax.psum(partial_value.astype(jnp.bfloat16), ("ffn", "sub")).astype(jnp.float32)
    hidden_units = (jax.nn.silu(summed[:, :unit_width]) * summed[:, unit_width:]).astype(
        jnp.bfloat16
    )
    ffn_total = lax.psum_scatter(
        jnp.dot(hidden_units, down_weight, preferred_element_type=jnp.float32).astype(jnp.bfloat16),
        "pool",
        scatter_dimension=0,
        tiled=True,
    ).astype(jnp.float32)
    return hidden_state + ffn_total


def fused_kernel(
    n_pool,
    q_hbm, k_hbm, v_hbm, nk_ref, nv_ref, len_ref, res_hbm, gain_ref, g_hbm, u_hbm, d_hbm,
    out_ref,
    qbuf, kbuf, vbuf, res, gw, uw, dw,
    qs, nkx, nvx, att, hid, xall, sqp, sqall,
    s1, r1, s2, r2, s3, r3, own, hall, acc, dsend, drecv,
    in_sem, w_sem, xs_sem, xr_sem, qs_sem, qr_sem, ts_sem, tr_sem,
    ps_sem, pr_sem, hs_sem, hr_sem, ds_sem, dr_sem,
):
    rows, width = qbuf.shape
    cap_len = kbuf.shape[1]
    kv_local = kbuf.shape[2] // HEAD_DIM
    heads = width // HEAD_DIM
    group_size = heads // kv_local
    units = hall.shape[3]
    half = rows // 2
    scaling = 1.0 / math.sqrt(HEAD_DIM)
    f32, bf16 = jnp.float32, jnp.bfloat16

    p = lax.axis_index("pool")
    f = lax.axis_index("ffn")
    s = lax.axis_index("sub")
    me = f * 2 + s
    pool_at = [lax.rem(p + d, n_pool) for d in range(1, n_pool)]
    sibling = {"sub": 1 - s}
    across = {"ffn": 1 - f}
    diagonal = {"ffn": 1 - f, "sub": 1 - s}
    near = [sibling, across, diagonal]

    def remote(src, dst, send, recv, to):
        return pltpu.make_async_remote_copy(
            src_ref=src, dst_ref=dst, send_sem=send, recv_sem=recv,
            device_id=to, device_id_type=MESH,
        )

    early = [
        pltpu.make_async_copy(q_hbm, qbuf, in_sem.at[0]),
        pltpu.make_async_copy(res_hbm, res, in_sem.at[1]),
    ]
    caches = []
    for c in range(2):
        at = pl.ds(c * half, half)
        caches.append(
            [
                pltpu.make_async_copy(k_hbm.at[at], kbuf.at[at], in_sem.at[2 + 2 * c]),
                pltpu.make_async_copy(v_hbm.at[at], vbuf.at[at], in_sem.at[3 + 2 * c]),
            ]
        )
    for copy in early + caches[0] + caches[1]:
        copy.start()
    weights = []
    for i, (src, dst) in enumerate(((g_hbm, gw), (u_hbm, uw), (d_hbm, dw))):
        step = src.shape[0] // 4
        weights.append(
            [
                pltpu.make_async_copy(
                    src.at[pl.ds(t * step, step)], dst.at[pl.ds(t * step, step)], w_sem.at[i, t]
                )
                for t in range(4)
            ]
        )

    barrier = pltpu.get_barrier_semaphore()
    for to in near + [{"pool": t} for t in pool_at]:
        pl.semaphore_signal(barrier, inc=1, device_id=to, device_id_type=MESH)

    for copy in early:
        copy.wait()
    for h in range(heads):
        kv = h // group_size
        qs[:, h, :] = qbuf[:, h * HEAD_DIM : (h + 1) * HEAD_DIM].astype(f32)
        nkx[:, h, :] = nk_ref[:, kv * HEAD_DIM : (kv + 1) * HEAD_DIM].astype(f32)
        nvx[:, h, :] = nv_ref[:, kv * HEAD_DIM : (kv + 1) * HEAD_DIM].astype(f32)

    batch = 8
    head_row = lax.broadcasted_iota(jnp.int32, (heads, HEAD_DIM), 0) // group_size
    lane = lax.broadcasted_iota(jnp.int32, (heads, cap_len), 1)

    def attend_batch(first):
        q3 = qs[pl.ds(first, batch)]
        self_score = jnp.sum(q3 * nkx[pl.ds(first, batch)], axis=2, keepdims=True) * scaling
        scores = []
        for b in range(batch):
            q = q3[b].astype(bf16)
            zero = jnp.zeros_like(q)
            wide = jnp.concatenate(
                [jnp.where(head_row == kv, q, zero) for kv in range(kv_local)], axis=1
            )
            raw = lax.dot_general(
                wide, kbuf[first + b], (((1,), (1,)), ((), ())), preferred_element_type=f32
            )
            scores.append(jnp.where(lane < len_ref[first + b], raw * scaling, -jnp.inf))
        scores = jnp.stack(scores)
        largest = jnp.maximum(jnp.max(scores, axis=2, keepdims=True), self_score)
        expo = jnp.exp(scores - largest)
        self_expo = jnp.exp(self_score - largest)
        totals = jnp.sum(expo, axis=2, keepdims=True) + self_expo
        weight = expo.astype(bf16)
        self_weight = self_expo.astype(bf16).astype(f32)
        mixed = []
        for b in range(batch):
            wide = jnp.dot(weight[b], vbuf[first + b], preferred_element_type=f32)
            one = wide[:, :HEAD_DIM]
            for kv in range(1, kv_local):
                one = jnp.where(
                    head_row == kv, wide[:, kv * HEAD_DIM : (kv + 1) * HEAD_DIM], one
                )
            mixed.append(one)
        mixed = jnp.stack(mixed) + self_weight * nvx[pl.ds(first, batch)]
        att[pl.ds(first, batch)] = mixed / totals

    gathers, started = ([], []), []
    for c in range(2):
        for copy in caches[c]:
            copy.wait()
        for copy in weights[c]:
            copy.start()

        @pl.loop(0, half // batch)
        def _(i):
            attend_batch(c * half + i * batch)

        at = pl.ds(c * half, half)
        mine = pl.ds(pl.multiple_of(p * half, half), half)
        squares = jnp.zeros((half, HEAD_DIM), f32)
        for h in range(heads):
            cols = pl.ds(h * HEAD_DIM, HEAD_DIM)
            state = res[at, cols] + att[at, h, :]
            hid[at, cols] = state
            squares = squares + state * state
            xall[c, mine, cols] = (state * gain_ref[:, cols]).astype(bf16)
        sqp[me, at] = jnp.broadcast_to(
            jnp.sum(squares, axis=1, keepdims=True), (half, HEAD_DIM)
        )
        if c == 0:
            pl.semaphore_wait(barrier, 3 + n_pool - 1)
        for d, to in enumerate(pool_at):
            copy = remote(
                xall.at[c, mine], xall.at[c, mine], xs_sem.at[c, d], xr_sem.at[c, d], {"pool": to}
            )
            copy.start()
            gathers[c].append(copy)
            started.append(copy)
    for copy in weights[2]:
        copy.start()

    parts_sent = [
        remote(sqp.at[me], sqp.at[me], qs_sem.at[i], qr_sem.at[i], to)
        for i, to in enumerate(near)
    ]
    for copy in parts_sent:
        copy.start()
    started.extend(parts_sent)
    sums_sent = [
        remote(sqall.at[p], sqall.at[p], ts_sem.at[d], tr_sem.at[d], {"pool": to})
        for d, to in enumerate(pool_at)
    ]
    started.extend(sums_sent)

    def spread_squares():
        for copy in parts_sent:
            copy.wait_recv()
        sqall[p] = sqp[0] + sqp[1] + sqp[2] + sqp[3]
        for copy in sums_sent:
            copy.start()

    pair = (gw, uw)
    sibling_unit, across_unit, diagonal_unit = f * 2 + 1 - s, (1 - f) * 2 + s, 3 - me
    awaited = ([], [])

    def part(c, w, j):
        return jnp.dot(
            xall[c],
            pair[w][:, pl.ds(pl.multiple_of(j * units, HEAD_DIM), units)],
            preferred_element_type=f32,
        )

    def reduce_out(c, w):
        s1[c, w] = part(c, w, diagonal_unit).astype(bf16)
        first = remote(s1.at[c, w], r1.at[c, w], ps_sem.at[c, 0, w], pr_sem.at[c, 0, w], sibling)
        first.start()
        value = part(c, w, across_unit)
        first.wait_recv()
        s2[c, w] = (value.astype(bf16).astype(f32) + r1[c, w].astype(f32)).astype(bf16)
        second = remote(s2.at[c, w], r2.at[c, w], ps_sem.at[c, 1, w], pr_sem.at[c, 1, w], across)
        second.start()
        started.extend([first, second])
        awaited[c].append(second)

    def reduce_in(c):
        for w in range(2):
            s3[c, w] = part(c, w, sibling_unit).astype(bf16)
            third = remote(
                s3.at[c, w], r3.at[c, w], ps_sem.at[c, 2, w], pr_sem.at[c, 2, w], sibling
            )
            third.start()
            started.append(third)
            awaited[c].append(third)
            own[c, w] = part(c, w, me).astype(bf16)

    def activate(c):
        squares = sqall[:, c * half : (c + 1) * half, :].reshape(n_pool * half, HEAD_DIM)
        scale = lax.rsqrt(squares[:, :1] / D + 1e-05)
        for copy in awaited[c]:
            copy.wait_recv()
        gate, up = [
            (own[c, w].astype(f32) + r3[c, w].astype(f32) + r2[c, w].astype(f32)) * scale
            for w in range(2)
        ]
        hall[c, me] = (gate / (1.0 + jnp.exp(-gate)) * up).astype(bf16)
        mine = hall.at[c, me]
        to_across = remote(mine, mine, hs_sem.at[c, 0], hr_sem.at[c, 0], across)
        to_sibling = remote(mine, mine, hs_sem.at[c, 1], hr_sem.at[c, 1], sibling)
        to_across.start()
        to_sibling.start()
        started.extend([to_across, to_sibling])
        return to_across, to_sibling

    tile = 512
    pieces = 2
    piece = width // pieces
    scattered = ([], [])

    def down(c, j, cols):
        return jnp.dot(
            hall[c, j],
            dw[pl.ds(pl.multiple_of(j * units, HEAD_DIM), units), cols],
            preferred_element_type=f32,
        )

    def column(i):
        return pl.ds(pl.multiple_of(i * tile, tile), tile)

    def project(c, to_across, to_sibling):
        @pl.loop(0, width // tile)
        def _(i):
            acc[:, column(i)] = down(c, me, column(i))

        to_sibling.wait_recv()

        @pl.loop(0, width // tile)
        def _(i):
            acc[:, column(i)] += down(c, sibling_unit, column(i))

        to_across.wait_recv()
        held = hall.at[c, across_unit]
        passed = remote(held, held, hs_sem.at[c, 2], hr_sem.at[c, 2], sibling)
        passed.start()
        started.append(passed)

        @pl.loop(0, width // tile)
        def _(i):
            acc[:, column(i)] += down(c, across_unit, column(i))

        passed.wait_recv()
        for i in range(pieces):

            @pl.loop(i * piece // tile, (i + 1) * piece // tile)
            def _(t):
                dsend[c, :, column(t)] = (
                    acc[:, column(t)] + down(c, diagonal_unit, column(t))
                ).astype(bf16)

            cols = pl.ds(i * piece, piece)
            for d, to in enumerate(pool_at):
                copy = remote(
                    dsend.at[c, pl.ds(pl.multiple_of(to * half, half), half), cols],
                    drecv.at[c, p, :, cols],
                    ds_sem.at[c, i, d], dr_sem.at[c, i, d], {"pool": to},
                )
                copy.start()
                scattered[c].append(copy)
                started.append(copy)
        drecv[c, p] = dsend[c, pl.ds(pl.multiple_of(p * half, half), half), :]

    def collect(c):
        at = pl.ds(c * half, half)
        far = n_pool - 1
        for i in range(pieces):
            cols = pl.ds(i * piece, piece)
            for copy in scattered[c][i * far : (i + 1) * far]:
                copy.wait_recv()
            total = drecv[c, 0, :, cols].astype(f32)
            for k in range(1, n_pool):
                total = total + drecv[c, k, :, cols].astype(f32)
            out_ref[at, cols] = hid[at, cols] + total

    def ready(copies):
        for copy in copies:
            copy.wait()

    def arrived(copies):
        for copy in copies:
            copy.wait_recv()

    ready(weights[0])
    arrived(gathers[0])
    reduce_out(0, 0)
    spread_squares()
    ready(weights[1])
    reduce_out(0, 1)
    reduce_in(0)
    arrived(gathers[1])
    reduce_out(1, 0)
    arrived(sums_sent)
    sent = activate(0)
    reduce_out(1, 1)
    reduce_in(1)
    ready(weights[2])
    project(0, *sent)
    sent = activate(1)
    project(1, *sent)
    collect(0)
    collect(1)
    for copy in started:
        copy.wait_send()


def fused_rows(
    n_pool, queries, cache_keys, cache_values, new_keys, new_values, kv_lengths,
    residual, norm_gain, gate_weight, up_weight, down_weight,
):
    rows, width = queries.shape
    every = n_pool * rows
    unit_width = gate_weight.shape[1]
    units = unit_width // 4
    heads = width // HEAD_DIM
    f32, bf16 = jnp.float32, jnp.bfloat16
    anywhere = pl.BlockSpec(memory_space=pl.ANY)
    vmem = pl.BlockSpec(memory_space=pltpu.VMEM)
    smem = pl.BlockSpec(memory_space=pltpu.SMEM)
    per_head = pltpu.VMEM((rows, heads, HEAD_DIM), f32)
    pair = pltpu.VMEM((2, 2, every // 2, units), bf16)
    dma = pltpu.SemaphoreType.DMA
    far = n_pool - 1
    return pl.pallas_call(
        functools.partial(fused_kernel, n_pool),
        out_shape=jax.ShapeDtypeStruct((rows, width), f32),
        in_specs=[anywhere] * 3 + [vmem] * 2 + [smem, anywhere, vmem] + [anywhere] * 3,
        out_specs=vmem,
        scratch_shapes=[
            pltpu.VMEM(queries.shape, bf16),
            pltpu.VMEM(cache_keys.shape, bf16),
            pltpu.VMEM(cache_values.shape, bf16),
            pltpu.VMEM(residual.shape, f32),
            pltpu.VMEM(gate_weight.shape, bf16),
            pltpu.VMEM(up_weight.shape, bf16),
            pltpu.VMEM(down_weight.shape, bf16),
            per_head, per_head, per_head, per_head,
            pltpu.VMEM((rows, width), f32),
            pltpu.VMEM((2, every // 2, width), bf16),
            pltpu.VMEM((4, rows, HEAD_DIM), f32),
            pltpu.VMEM((n_pool, rows, HEAD_DIM), f32),
            pair, pair, pair, pair, pair, pair, pair,
            pltpu.VMEM((2, 4, every // 2, units), bf16),
            pltpu.VMEM((every // 2, width), f32),
            pltpu.VMEM((2, every // 2, width), bf16),
            pltpu.VMEM((2, n_pool, rows // 2, width), bf16),
            dma((6,)), dma((3, 4)),
            dma((2, far)), dma((2, far)), dma((3,)), dma((3,)), dma((far,)), dma((far,)),
            dma((2, 3, 2)), dma((2, 3, 2)), dma((2, 3)), dma((2, 3)),
            dma((2, 2, far)), dma((2, 2, far)),
        ],
        compiler_params=pltpu.CompilerParams(
            collective_id=0, has_side_effects=True, vmem_limit_bytes=VMEM_BYTES
        ),
    )(
        queries, cache_keys, cache_values, new_keys, new_values, kv_lengths, residual,
        norm_gain.reshape(1, width), gate_weight, up_weight, down_weight,
    )


def fits(n_pool, n_ffn, n_sub, queries, cache_keys, gate_weight, down_weight):
    rows, width = queries.shape
    unit_width = gate_weight.shape[1]
    weight_bytes = 2 * (2 * gate_weight.size + down_weight.size)
    return (
        n_ffn == 2
        and n_sub == 2
        and n_pool > 1
        and rows % 32 == 0
        and width % 1024 == 0
        and unit_width % (4 * HEAD_DIM) == 0
        and weight_bytes + 4 * cache_keys.size + 24 * n_pool * rows * unit_width
        <= VMEM_BYTES
    )


def on_device(mesh_shape, *operands):
    n_pool, n_ffn, n_sub = mesh_shape["pool"], mesh_shape["ffn"], mesh_shape["sub"]
    queries, cache_keys = operands[0], operands[1]
    if fits(n_pool, n_ffn, n_sub, queries, cache_keys, operands[8], operands[10]):
        return fused_rows(n_pool, *operands)
    return layer_rows(*operands)


def solution(mesh):
    placed = (
        P(("groups", "pool"), ("ffn", "sub")),
        P(("groups", "pool"), None, ("ffn", "sub")),
        P(("groups", "pool"), None, ("ffn", "sub")),
        P(("groups", "pool"), ("ffn", "sub")),
        P(("groups", "pool"), ("ffn", "sub")),
        P(("groups", "pool")),
        P(("groups", "pool"), ("ffn", "sub")),
        P(("ffn", "sub")),
        P(("ffn", "sub"), "pool"),
        P(("ffn", "sub"), "pool"),
        P("pool", ("ffn", "sub")),
    )
    return jax.shard_map(
        functools.partial(on_device, dict(mesh.shape)),
        mesh=mesh,
        in_specs=placed,
        out_specs=P(("groups", "pool"), ("ffn", "sub")),
        check_vma=False,
    )
```

```python
import functools
import math

import jax
import jax.numpy as jnp
from jax import lax
from jax.experimental import pallas as pl
from jax.experimental.pallas import tpu as pltpu
from jax.sharding import PartitionSpec as P

HEAD_DIM = 128
D = 8192
MESH = pl.DeviceIdType.MESH
VMEM_BYTES = 60 * 1024 * 1024


def rounded(values):
    return lax.optimization_barrier(values.astype(jnp.bfloat16)).astype(jnp.float32)


def attend(queries, cache_keys, cache_values, new_keys, new_values, kv_lengths):
    row_count, cap_len, kv_width = cache_keys.shape
    kv_local = kv_width // HEAD_DIM
    group_size = queries.shape[1] // kv_width
    scaling = 1.0 / math.sqrt(HEAD_DIM)
    query_heads = queries.reshape(row_count, kv_local, group_size, HEAD_DIM)
    key_heads = cache_keys.reshape(row_count, cap_len, kv_local, HEAD_DIM)
    value_heads = cache_values.reshape(row_count, cap_len, kv_local, HEAD_DIM)
    scores = (
        jnp.einsum("rhgd,rchd->rhgc", query_heads, key_heads, preferred_element_type=jnp.float32)
        * scaling
    )
    self_score = (
        jnp.einsum(
            "rhgd,rhd->rhg",
            query_heads,
            new_keys.reshape(row_count, kv_local, HEAD_DIM),
            preferred_element_type=jnp.float32,
        )
        * scaling
    )
    live_mask = lax.broadcasted_iota(jnp.int32, (row_count, cap_len), 1) < kv_lengths[:, None]
    scores = jnp.where(live_mask[:, None, None, :], scores, -jnp.inf)
    largest = jnp.maximum(jnp.max(scores, axis=3), self_score)
    expo = jnp.exp(scores - largest[..., None])
    self_expo = jnp.exp(self_score - largest)
    totals = jnp.sum(expo, axis=3) + self_expo
    mixed = jnp.einsum(
        "rhgc,rchd->rhgd",
        expo.astype(jnp.bfloat16),
        value_heads,
        preferred_element_type=jnp.float32,
    )
    mixed = mixed + rounded(self_expo)[..., None] * new_values.reshape(
        row_count, kv_local, 1, HEAD_DIM
    ).astype(jnp.float32)
    return (mixed / totals[..., None]).reshape(row_count, kv_local * group_size * HEAD_DIM)


def layer_rows(
    queries,
    cache_keys,
    cache_values,
    new_keys,
    new_values,
    kv_lengths,
    residual,
    norm_gain,
    gate_weight,
    up_weight,
    down_weight,
):
    hidden_state = residual + attend(
        queries, cache_keys, cache_values, new_keys, new_values, kv_lengths
    )
    squares = lax.psum(jnp.sum(hidden_state * hidden_state, axis=1), ("ffn", "sub"))
    normed = (hidden_state * lax.rsqrt(squares / D + 1e-05)[:, None] * norm_gain[None, :]).astype(
        jnp.bfloat16
    )
    unit_width = gate_weight.shape[1]
    block_rows = lax.all_gather(normed, "pool", axis=0, tiled=True)
    gate_part = jnp.dot(block_rows, gate_weight, preferred_element_type=jnp.float32)
    up_part = jnp.dot(block_rows, up_weight, preferred_element_type=jnp.float32)
    partial_value = jnp.concatenate([gate_part, up_part], axis=1)
    summed = lax.psum(partial_value.astype(jnp.bfloat16), ("ffn", "sub")).astype(jnp.float32)
    hidden_units = (jax.nn.silu(summed[:, :unit_width]) * summed[:, unit_width:]).astype(
        jnp.bfloat16
    )
    ffn_total = lax.psum_scatter(
        jnp.dot(hidden_units, down_weight, preferred_element_type=jnp.float32).astype(jnp.bfloat16),
        "pool",
        scatter_dimension=0,
        tiled=True,
    ).astype(jnp.float32)
    return hidden_state + ffn_total


def fused_kernel(
    n_pool,
    q_hbm, k_hbm, v_hbm, nk_ref, nv_ref, len_ref, res_hbm, gain_ref, g_hbm, u_hbm, d_hbm,
    out_ref,
    qbuf, kbuf, vbuf, res, gw, uw, dw,
    qs, nkx, nvx, att, hid, xall, sqp, sqall,
    s1, r1, s2, r2, s3, r3, own, hall, acc, dsend, drecv,
    in_sem, w_sem, xs_sem, xr_sem, qs_sem, qr_sem, ts_sem, tr_sem,
    ps_sem, pr_sem, hs_sem, hr_sem, ds_sem, dr_sem,
):
    rows, width = qbuf.shape
    cap_len = kbuf.shape[1]
    kv_local = kbuf.shape[2] // HEAD_DIM
    heads = width // HEAD_DIM
    group_size = heads // kv_local
    units = hall.shape[3]
    half = rows // 2
    scaling = 1.0 / math.sqrt(HEAD_DIM)
    f32, bf16 = jnp.float32, jnp.bfloat16

    p = lax.axis_index("pool")
    f = lax.axis_index("ffn")
    s = lax.axis_index("sub")
    me = f * 2 + s
    if n_pool == 4:
        pool_at = [3 - p, lax.rem(p + 2, 4), p + 1 - 2 * lax.rem(p, 2)]
    else:
        pool_at = [lax.rem(p + d, n_pool) for d in range(1, n_pool)]
    sibling = {"sub": 1 - s}
    across = {"ffn": 1 - f}
    diagonal = {"ffn": 1 - f, "sub": 1 - s}
    near = [sibling, across, diagonal]

    def remote(src, dst, send, recv, to):
        return pltpu.make_async_remote_copy(
            src_ref=src, dst_ref=dst, send_sem=send, recv_sem=recv,
            device_id=to, device_id_type=MESH,
        )

    early = [
        pltpu.make_async_copy(q_hbm, qbuf, in_sem.at[0]),
        pltpu.make_async_copy(res_hbm, res, in_sem.at[1]),
    ]
    caches = []
    for c in range(2):
        at = pl.ds(c * half, half)
        caches.append(
            [
                pltpu.make_async_copy(k_hbm.at[at], kbuf.at[at], in_sem.at[2 + 2 * c]),
                pltpu.make_async_copy(v_hbm.at[at], vbuf.at[at], in_sem.at[3 + 2 * c]),
            ]
        )
    for copy in early + caches[0] + caches[1]:
        copy.start()
    weights = []
    for i, (src, dst) in enumerate(((g_hbm, gw), (u_hbm, uw), (d_hbm, dw))):
        step = src.shape[0] // 4
        weights.append(
            [
                pltpu.make_async_copy(
                    src.at[pl.ds(t * step, step)], dst.at[pl.ds(t * step, step)], w_sem.at[i, t]
                )
                for t in range(4)
            ]
        )

    barrier = pltpu.get_barrier_semaphore()
    for to in near + [{"pool": t} for t in pool_at]:
        pl.semaphore_signal(barrier, inc=1, device_id=to, device_id_type=MESH)

    for copy in early:
        copy.wait()
    for h in range(heads):
        kv = h // group_size
        qs[:, h, :] = qbuf[:, h * HEAD_DIM : (h + 1) * HEAD_DIM].astype(f32)
        nkx[:, h, :] = nk_ref[:, kv * HEAD_DIM : (kv + 1) * HEAD_DIM].astype(f32)
        nvx[:, h, :] = nv_ref[:, kv * HEAD_DIM : (kv + 1) * HEAD_DIM].astype(f32)

    batch = 8
    head_row = lax.broadcasted_iota(jnp.int32, (heads, HEAD_DIM), 0) // group_size
    lane = lax.broadcasted_iota(jnp.int32, (heads, cap_len), 1)

    def attend_batch(first):
        q3 = qs[pl.ds(first, batch)]
        self_score = jnp.sum(q3 * nkx[pl.ds(first, batch)], axis=2, keepdims=True) * scaling
        scores = []
        for b in range(batch):
            q = q3[b].astype(bf16)
            zero = jnp.zeros_like(q)
            wide = jnp.concatenate(
                [jnp.where(head_row == kv, q, zero) for kv in range(kv_local)], axis=1
            )
            raw = lax.dot_general(
                wide, kbuf[first + b], (((1,), (1,)), ((), ())), preferred_element_type=f32
            )
            scores.append(jnp.where(lane < len_ref[first + b], raw * scaling, -jnp.inf))
        scores = jnp.stack(scores)
        largest = jnp.maximum(jnp.max(scores, axis=2, keepdims=True), self_score)
        expo = jnp.exp(scores - largest)
        self_expo = jnp.exp(self_score - largest)
        totals = jnp.sum(expo, axis=2, keepdims=True) + self_expo
        weight = expo.astype(bf16)
        self_weight = self_expo.astype(bf16).astype(f32)
        mixed = []
        for b in range(batch):
            wide = jnp.dot(weight[b], vbuf[first + b], preferred_element_type=f32)
            one = wide[:, :HEAD_DIM]
            for kv in range(1, kv_local):
                one = jnp.where(
                    head_row == kv, wide[:, kv * HEAD_DIM : (kv + 1) * HEAD_DIM], one
                )
            mixed.append(one)
        mixed = jnp.stack(mixed) + self_weight * nvx[pl.ds(first, batch)]
        att[pl.ds(first, batch)] = mixed / totals

    gathers, started = ([], []), []
    for c in range(2):
        for copy in caches[c]:
            copy.wait()
        for copy in weights[c]:
            copy.start()

        @pl.loop(0, half // batch)
        def _(i):
            attend_batch(c * half + i * batch)

        at = pl.ds(c * half, half)
        mine = pl.ds(pl.multiple_of(p * half, half), half)
        squares = jnp.zeros((half, HEAD_DIM), f32)
        for h in range(heads):
            cols = pl.ds(h * HEAD_DIM, HEAD_DIM)
            state = res[at, cols] + att[at, h, :]
            hid[at, cols] = state
            squares = squares + state * state
            xall[c, mine, cols] = (state * gain_ref[:, cols]).astype(bf16)
        sqp[me, at] = jnp.broadcast_to(
            jnp.sum(squares, axis=1, keepdims=True), (half, HEAD_DIM)
        )
        if c == 0:
            pl.semaphore_wait(barrier, 3 + n_pool - 1)
        for d, to in enumerate(pool_at):
            copy = remote(
                xall.at[c, mine], xall.at[c, mine], xs_sem.at[c, d], xr_sem.at[c, d], {"pool": to}
            )
            copy.start()
            gathers[c].append(copy)
            started.append(copy)
    for copy in weights[2]:
        copy.start()

    parts_sent = [
        remote(sqp.at[me], sqp.at[me], qs_sem.at[i], qr_sem.at[i], to)
        for i, to in enumerate(near)
    ]
    for copy in parts_sent:
        copy.start()
    started.extend(parts_sent)
    sums_sent = [
        remote(sqall.at[p], sqall.at[p], ts_sem.at[d], tr_sem.at[d], {"pool": to})
        for d, to in enumerate(pool_at)
    ]
    started.extend(sums_sent)

    def spread_squares():
        for copy in parts_sent:
            copy.wait_recv()
        sqall[p] = sqp[0] + sqp[1] + sqp[2] + sqp[3]
        for copy in sums_sent:
            copy.start()

    pair = (gw, uw)
    sibling_unit, across_unit, diagonal_unit = f * 2 + 1 - s, (1 - f) * 2 + s, 3 - me
    awaited = ([], [])

    def part(c, w, j):
        return jnp.dot(
            xall[c],
            pair[w][:, pl.ds(pl.multiple_of(j * units, HEAD_DIM), units)],
            preferred_element_type=f32,
        )

    def reduce_out(c, w):
        s1[c, w] = part(c, w, diagonal_unit).astype(bf16)
        first = remote(s1.at[c, w], r1.at[c, w], ps_sem.at[c, 0, w], pr_sem.at[c, 0, w], sibling)
        first.start()
        value = part(c, w, across_unit)
        first.wait_recv()
        s2[c, w] = (value.astype(bf16).astype(f32) + r1[c, w].astype(f32)).astype(bf16)
        second = remote(s2.at[c, w], r2.at[c, w], ps_sem.at[c, 1, w], pr_sem.at[c, 1, w], across)
        second.start()
        started.extend([first, second])
        awaited[c].append(second)

    def reduce_in(c):
        for w in range(2):
            s3[c, w] = part(c, w, sibling_unit).astype(bf16)
            third = remote(
                s3.at[c, w], r3.at[c, w], ps_sem.at[c, 2, w], pr_sem.at[c, 2, w], sibling
            )
            third.start()
            started.append(third)
            awaited[c].append(third)
            own[c, w] = part(c, w, me).astype(bf16)

    def activate(c):
        squares = sqall[:, c * half : (c + 1) * half, :].reshape(n_pool * half, HEAD_DIM)
        scale = lax.rsqrt(squares[:, :1] / D + 1e-05)
        for copy in awaited[c]:
            copy.wait_recv()
        gate, up = [
            (own[c, w].astype(f32) + r3[c, w].astype(f32) + r2[c, w].astype(f32)) * scale
            for w in range(2)
        ]
        hall[c, me] = (gate / (1.0 + jnp.exp(-gate)) * up).astype(bf16)
        mine = hall.at[c, me]
        to_across = remote(mine, mine, hs_sem.at[c, 0], hr_sem.at[c, 0], across)
        to_sibling = remote(mine, mine, hs_sem.at[c, 1], hr_sem.at[c, 1], sibling)
        to_across.start()
        to_sibling.start()
        started.extend([to_across, to_sibling])
        return to_across, to_sibling

    tile = 512
    pieces = 2
    piece = width // pieces
    scattered = ([], [])

    def down(c, j, cols):
        return jnp.dot(
            hall[c, j],
            dw[pl.ds(pl.multiple_of(j * units, HEAD_DIM), units), cols],
            preferred_element_type=f32,
        )

    def column(i):
        return pl.ds(pl.multiple_of(i * tile, tile), tile)

    def project(c, to_across, to_sibling):
        @pl.loop(0, width // tile)
        def _(i):
            acc[:, column(i)] = down(c, me, column(i))

        to_sibling.wait_recv()

        @pl.loop(0, width // tile)
        def _(i):
            acc[:, column(i)] += down(c, sibling_unit, column(i))

        to_across.wait_recv()
        held = hall.at[c, across_unit]
        passed = remote(held, held, hs_sem.at[c, 2], hr_sem.at[c, 2], sibling)
        passed.start()
        started.append(passed)

        @pl.loop(0, width // tile)
        def _(i):
            acc[:, column(i)] += down(c, across_unit, column(i))

        passed.wait_recv()
        for i in range(pieces):

            @pl.loop(i * piece // tile, (i + 1) * piece // tile)
            def _(t):
                dsend[c, :, column(t)] = (
                    acc[:, column(t)] + down(c, diagonal_unit, column(t))
                ).astype(bf16)

            cols = pl.ds(i * piece, piece)
            for d, to in enumerate(pool_at):
                copy = remote(
                    dsend.at[c, pl.ds(pl.multiple_of(to * half, half), half), cols],
                    drecv.at[c, p, :, cols],
                    ds_sem.at[c, i, d], dr_sem.at[c, i, d], {"pool": to},
                )
                copy.start()
                scattered[c].append(copy)
                started.append(copy)
        drecv[c, p] = dsend[c, pl.ds(pl.multiple_of(p * half, half), half), :]

    def collect(c):
        at = pl.ds(c * half, half)
        far = n_pool - 1
        for i in range(pieces):
            cols = pl.ds(i * piece, piece)
            for copy in scattered[c][i * far : (i + 1) * far]:
                copy.wait_recv()
            total = drecv[c, 0, :, cols].astype(f32)
            for k in range(1, n_pool):
                total = total + drecv[c, k, :, cols].astype(f32)
            out_ref[at, cols] = hid[at, cols] + total

    def ready(copies):
        for copy in copies:
            copy.wait()

    def arrived(copies):
        for copy in copies:
            copy.wait_recv()

    ready(weights[0])
    arrived(gathers[0])
    reduce_out(0, 0)
    spread_squares()
    ready(weights[1])
    reduce_out(0, 1)
    reduce_in(0)
    arrived(gathers[1])
    reduce_out(1, 0)
    arrived(sums_sent)
    sent = activate(0)
    reduce_out(1, 1)
    reduce_in(1)
    ready(weights[2])
    project(0, *sent)
    sent = activate(1)
    project(1, *sent)
    collect(0)
    collect(1)
    for copy in started:
        copy.wait_send()


def fused_rows(
    n_pool, queries, cache_keys, cache_values, new_keys, new_values, kv_lengths,
    residual, norm_gain, gate_weight, up_weight, down_weight,
):
    rows, width = queries.shape
    every = n_pool * rows
    unit_width = gate_weight.shape[1]
    units = unit_width // 4
    heads = width // HEAD_DIM
    f32, bf16 = jnp.float32, jnp.bfloat16
    anywhere = pl.BlockSpec(memory_space=pl.ANY)
    vmem = pl.BlockSpec(memory_space=pltpu.VMEM)
    smem = pl.BlockSpec(memory_space=pltpu.SMEM)
    per_head = pltpu.VMEM((rows, heads, HEAD_DIM), f32)
    pair = pltpu.VMEM((2, 2, every // 2, units), bf16)
    dma = pltpu.SemaphoreType.DMA
    far = n_pool - 1
    return pl.pallas_call(
        functools.partial(fused_kernel, n_pool),
        out_shape=jax.ShapeDtypeStruct((rows, width), f32),
        in_specs=[anywhere] * 3 + [vmem] * 2 + [smem, anywhere, vmem] + [anywhere] * 3,
        out_specs=vmem,
        scratch_shapes=[
            pltpu.VMEM(queries.shape, bf16),
            pltpu.VMEM(cache_keys.shape, bf16),
            pltpu.VMEM(cache_values.shape, bf16),
            pltpu.VMEM(residual.shape, f32),
            pltpu.VMEM(gate_weight.shape, bf16),
            pltpu.VMEM(up_weight.shape, bf16),
            pltpu.VMEM(down_weight.shape, bf16),
            per_head, per_head, per_head, per_head,
            pltpu.VMEM((rows, width), f32),
            pltpu.VMEM((2, every // 2, width), bf16),
            pltpu.VMEM((4, rows, HEAD_DIM), f32),
            pltpu.VMEM((n_pool, rows, HEAD_DIM), f32),
            pair, pair, pair, pair, pair, pair, pair,
            pltpu.VMEM((2, 4, every // 2, units), bf16),
            pltpu.VMEM((every // 2, width), f32),
            pltpu.VMEM((2, every // 2, width), bf16),
            pltpu.VMEM((2, n_pool, rows // 2, width), bf16),
            dma((6,)), dma((3, 4)),
            dma((2, far)), dma((2, far)), dma((3,)), dma((3,)), dma((far,)), dma((far,)),
            dma((2, 3, 2)), dma((2, 3, 2)), dma((2, 3)), dma((2, 3)),
            dma((2, 2, far)), dma((2, 2, far)),
        ],
        compiler_params=pltpu.CompilerParams(
            collective_id=0, has_side_effects=True, vmem_limit_bytes=VMEM_BYTES
        ),
    )(
        queries, cache_keys, cache_values, new_keys, new_values, kv_lengths, residual,
        norm_gain.reshape(1, width), gate_weight, up_weight, down_weight,
    )


def fits(n_pool, n_ffn, n_sub, queries, cache_keys, gate_weight, down_weight):
    rows, width = queries.shape
    unit_width = gate_weight.shape[1]
    weight_bytes = 2 * (2 * gate_weight.size + down_weight.size)
    return (
        n_ffn == 2
        and n_sub == 2
        and n_pool > 1
        and rows % 32 == 0
        and width % 1024 == 0
        and unit_width % (4 * HEAD_DIM) == 0
        and weight_bytes + 4 * cache_keys.size + 24 * n_pool * rows * unit_width
        <= VMEM_BYTES
    )


def on_device(mesh_shape, *operands):
    n_pool, n_ffn, n_sub = mesh_shape["pool"], mesh_shape["ffn"], mesh_shape["sub"]
    queries, cache_keys = operands[0], operands[1]
    if fits(n_pool, n_ffn, n_sub, queries, cache_keys, operands[8], operands[10]):
        return fused_rows(n_pool, *operands)
    return layer_rows(*operands)


def solution(mesh):
    placed = (
        P(("groups", "pool"), ("ffn", "sub")),
        P(("groups", "pool"), None, ("ffn", "sub")),
        P(("groups", "pool"), None, ("ffn", "sub")),
        P(("groups", "pool"), ("ffn", "sub")),
        P(("groups", "pool"), ("ffn", "sub")),
        P(("groups", "pool")),
        P(("groups", "pool"), ("ffn", "sub")),
        P(("ffn", "sub")),
        P(("ffn", "sub"), "pool"),
        P(("ffn", "sub"), "pool"),
        P("pool", ("ffn", "sub")),
    )
    return jax.shard_map(
        functools.partial(on_device, dict(mesh.shape)),
        mesh=mesh,
        in_specs=placed,
        out_specs=P(("groups", "pool"), ("ffn", "sub")),
        check_vma=False,
    )
```
